256 devices in a mesh: row: 8 (over x, y_lo), col: 16 (over z, core), slab: 2 (over y_hi).
Axes of the slice: x: 4, y: 4 (y_hi: 2, y_lo: 2; y = y_hi * 2 + y_lo), z: 8, core: 2. Of those that a mesh axis runs over, the one named last changes fastest.
Arguments:
- iterate: bfloat16 [4096, 9216], P(('row', 'col'), 'slab'), as said below
Outputs:
- update: bfloat16 [4096, 9216], P(('row', 'col'), 'slab')
Inputs may be any that keep to these rules, and one draw needn't show every extreme that they name: `iterate`: entries lie within plus or minus 3 / sqrt(9216).
All inputs are finite; a program needn't handle non-finite values.
Results may differ from the reference program's by a relative error of at most 0.0056.
Values may be sent and summed in bfloat16 or wider, within the bound.
No kernel may reach another device: no remote copies, remote signals or barrier semaphores. Data moves between devices by JAX's collectives and lax.ppermute only.
A program may use at most 64 MiB of HBM per device.

```python
import math
import jax
import jax.numpy as jnp

M = 4096
NC = 9216


def draw_iterate(key, part):
    key = jax.random.fold_in(key, 7)
    spread = 0.7 / math.sqrt(NC)
    values = jax.random.truncated_normal(key, -4.0, 4.0, (M, NC), jnp.float32)
    return (spread * values).astype(jnp.bfloat16)


def setup_inputs(seed: int = 0) -> dict:
    keys = jax.random.split(jax.random.key(seed), 2)
    return {
        "iterate": draw_iterate(jax.random.fold_in(keys[1], 71), 0),
    }


coef_linear = 3.4445
coef_cubic = -4.775
coef_quintic = 2.0315
update_gain = 0.2 * math.sqrt(18432.0)

def reference(iterate):
    gram_matrix = jnp.dot(iterate, iterate.T, preferred_element_type=jnp.float32).astype(jnp.bfloat16)
    squared = jnp.dot(gram_matrix, gram_matrix, preferred_element_type=jnp.float32)
    polynomial = (coef_cubic * gram_matrix.astype(jnp.float32) + coef_quintic * squared).astype(jnp.bfloat16)
    applied = jnp.dot(polynomial, iterate, preferred_element_type=jnp.float32)
    stepped = coef_linear * iterate.astype(jnp.float32) + applied
    return (update_gain * stepped).astype(jnp.bfloat16)
```

```python
import math

import jax
import jax.numpy as jnp
from jax import lax
from jax.sharding import Mesh
from jax.sharding import PartitionSpec as P

coef_linear = 3.4445
coef_cubic = -4.775
coef_quintic = 2.0315
update_gain = 0.2 * math.sqrt(18432.0)

X, YL, Z, C, S = "x", "yl", "z", "c", "s"
NZ, NR = 8, 8
bf16, f32 = jnp.bfloat16, jnp.float32
COLS_Z = 768


def swap(a, axis):
    return lax.ppermute(a, axis, [(0, 1), (1, 0)])


def shift(a, axis, n, d):
    return lax.ppermute(a, axis, [((i + d) % n, i) for i in range(n)])


def ring_z(a):
    out = [None] * NZ
    out[0] = up = down = a
    for step in range(1, 4):
        up = shift(up, Z, NZ, 1)
        down = shift(down, Z, NZ, -1)
        out[step], out[NZ - step] = up, down
    half = a.shape[0] // 2
    out[4] = jnp.concatenate([shift(up[:half], Z, NZ, 1), shift(down[half:], Z, NZ, -1)])
    return out


def gather_r(a):
    copies = jnp.broadcast_to(a[None], (NR, *a.shape))
    return lax.all_to_all(copies, (X, YL), 0, 0, tiled=True)


def dot_t(a, b):
    return lax.dot_general(a, b, (((1,), (1,)), ((), ())), preferred_element_type=f32)


def on_device(iterate):
    core, z = lax.axis_index(C), lax.axis_index(Z)
    mine = lax.all_to_all(iterate, C, 1, 0, tiled=True)
    x_rows = lax.all_gather(mine, Z, axis=0, tiled=True)
    x_cols = gather_r(mine)
    halves = [x_cols[:, 32 * h : 32 * h + 32].reshape(256, -1) for h in (0, 1)]
    part = [dot_t(x_rows, h) for h in halves]

    first = core == 0
    own = jnp.where(first, part[0], part[1])
    other = jnp.where(first, part[1], part[0]).astype(bf16)
    own = own + swap(other, C).astype(f32)
    sent = own.astype(bf16)
    gram = (own + swap(sent, S).astype(f32)).astype(bf16)
    gram_o = swap(gram, C)
    g0 = jnp.where(first, gram, gram_o)
    g1 = jnp.where(first, gram_o, gram)
    tile = jnp.concatenate([g0, g1], axis=1)
    rows = lax.dynamic_index_in_dim(tile.reshape(NZ, 2, 32, 512), core, 1, keepdims=False)
    row_block = rows.reshape(256, 512)

    a_shards = ring_z(gram)
    b_all = gather_r(row_block).reshape(NR, NZ, 32, 512)
    squared = jnp.zeros((512, 512), f32)
    for d in range(NZ):
        b = lax.dynamic_index_in_dim(b_all, (z + d) % NZ, 1, keepdims=False).reshape(256, 512)
        squared = squared + jnp.dot(a_shards[d], b, preferred_element_type=f32)
    squared = squared + swap(squared.astype(bf16), C).astype(f32)
    poly = (coef_cubic * tile.astype(f32) + coef_quintic * squared).astype(bf16)

    x_ord = jnp.concatenate(halves, axis=0)
    part_z = jnp.dot(poly, x_ord[:, :COLS_Z], preferred_element_type=f32).astype(bf16)
    sum_z = lax.psum_scatter(part_z, Z, scatter_dimension=0, tiled=True).astype(f32)
    part_r = lax.dot_general(
        poly, x_rows[:, COLS_Z:], (((0,), (0,)), ((), ())), preferred_element_type=f32
    ).astype(bf16)
    part_r = part_r.reshape(2, NR, 32, -1).transpose(1, 0, 2, 3)
    sum_r = lax.all_to_all(part_r, (X, YL), 0, 0, tiled=True).astype(f32).sum(0).reshape(64, -1)
    applied = jnp.concatenate([sum_z, sum_r], axis=1)
    stepped = coef_linear * mine.astype(f32) + applied
    out = (update_gain * stepped).astype(bf16)
    return lax.all_to_all(out, C, 0, 1, tiled=True)


def solution(mesh):
    fine = Mesh(mesh.devices.reshape(4, 2, 8, 2, 2), (X, YL, Z, C, S))
    spec = P((X, YL, Z, C), S)
    return jax.shard_map(on_device, mesh=fine, in_specs=(spec,), out_specs=spec, check_vma=False)
```

```python
import math

import jax
import jax.numpy as jnp
from jax import lax
from jax.sharding import Mesh
from jax.sharding import PartitionSpec as P

coef_linear = 3.4445
coef_cubic = -4.775
coef_quintic = 2.0315
update_gain = 0.2 * math.sqrt(18432.0)

X, YL, Z, C, S = "x", "yl", "z", "c", "s"
NZ, NR = 8, 8
bf16, f32 = jnp.bfloat16, jnp.float32
COLS_Z = 768


def swap(a):
    return lax.ppermute(a, C, [(0, 1), (1, 0)])


def swap_slab(a):
    return lax.ppermute(a, S, [(0, 1), (1, 0)])


def shift_z(a, d):
    return lax.ppermute(a, Z, [((i + d) % NZ, i) for i in range(NZ)])


def turn(a):
    pairs = []
    for i in range(NZ):
        pairs += [(2 * ((i + 1) % NZ), 2 * i), (2 * ((i - 1) % NZ) + 1, 2 * i + 1)]
    return lax.ppermute(a, (Z, C), pairs)


def ring_z(a, b):
    out = [a] + [None] * (NZ - 1)
    for step in range(1, 4):
        a = turn(a)
        b = turn(b)
        out[step], out[NZ - step] = a, swap(b)
    out[4] = turn(a)
    return out


def gather_r(a):
    copies = jnp.broadcast_to(a[None], (NR, *a.shape))
    return lax.all_to_all(copies, (X, YL), 0, 0, tiled=True)


def dot_t(a, b):
    return lax.dot_general(a, b, (((1,), (1,)), ((), ())), preferred_element_type=f32)


def on_device(iterate):
    core, z = lax.axis_index(C), lax.axis_index(Z)
    first = core == 0
    left, right = iterate[:, :2304], iterate[:, 2304:]
    got = swap(jnp.where(first, right, left))
    mine = jnp.concatenate([jnp.where(first, left, got), jnp.where(first, got, right)], axis=0)
    x_rows = lax.all_gather(mine, Z, axis=0, tiled=True)
    x_cols = gather_r(mine)
    halves = [x_cols[:, 32 * h : 32 * h + 32].reshape(256, -1) for h in (0, 1)]
    part = [dot_t(x_rows, h) for h in halves]

    own = jnp.where(first, part[0], part[1])
    other = jnp.where(first, part[1], part[0]).astype(bf16)
    own = own + swap(other).astype(f32)
    sent = own.astype(bf16)
    gram = (own + swap_slab(sent).astype(f32)).astype(bf16)
    gram_o = swap(gram)
    g0 = jnp.where(first, gram, gram_o)
    g1 = jnp.where(first, gram_o, gram)
    tile = jnp.concatenate([g0, g1], axis=1)
    rows = lax.dynamic_index_in_dim(tile.reshape(NZ, 2, 32, 512), core, 1, keepdims=False)
    row_block = rows.reshape(256, 512)

    a_shards = ring_z(gram, gram_o)
    b_all = gather_r(row_block).reshape(NR, NZ, 32, 512)
    up = 1 - 2 * core
    squared = jnp.zeros((512, 512), f32)
    for e in range(NZ):
        at = (z + up * e + NZ) % NZ
        b = lax.dynamic_index_in_dim(b_all, at, 1, keepdims=False).reshape(256, 512)
        squared = squared + jnp.dot(a_shards[e], b, preferred_element_type=f32)
    squared = squared + swap(squared.astype(bf16)).astype(f32)
    poly = (coef_cubic * tile.astype(f32) + coef_quintic * squared).astype(bf16)

    x_ord = jnp.concatenate(halves, axis=0)
    part_z = jnp.dot(poly, x_ord[:, :COLS_Z], preferred_element_type=f32).astype(bf16)
    part_z = part_z.reshape(NZ, 64, COLS_Z)
    take = lambda d: lax.dynamic_index_in_dim(part_z, (z - d + NZ) % NZ, 0, keepdims=False)
    got_z = [shift_z(take(d), d) for d in (4, 1, 7, 2, 6, 3, 5)]
    part_r = lax.dot_general(
        poly, x_rows[:, COLS_Z:], (((0,), (0,)), ((), ())), preferred_element_type=f32
    ).astype(bf16)
    part_r = part_r.reshape(2, NR, 32, -1).transpose(1, 0, 2, 3)
    got_r = lax.all_to_all(part_r, (X, YL), 0, 0, tiled=True)
    sum_z = sum([p.astype(f32) for p in got_z], take(0).astype(f32))
    sum_r = got_r.astype(f32).sum(0).reshape(64, -1)
    applied = jnp.concatenate([sum_z, sum_r], axis=1)
    stepped = coef_linear * mine.astype(f32) + applied
    out = (update_gain * stepped).astype(bf16)
    up_rows, low_rows = out[:32], out[32:]
    got = swap(jnp.where(first, low_rows, up_rows))
    own = jnp.where(first, up_rows, low_rows)
    return jnp.concatenate([jnp.where(first, own, got), jnp.where(first, got, own)], axis=1)


def solution(mesh):
    fine = Mesh(mesh.devices.reshape(4, 2, 8, 2, 2), (X, YL, Z, C, S))
    spec = P((X, YL, Z, C), S)
    return jax.shard_map(on_device, mesh=fine, in_specs=(spec,), out_specs=spec, check_vma=False)
```

```python
import math

import jax
import jax.numpy as jnp
from jax import lax
from jax.sharding import Mesh
from jax.sharding import PartitionSpec as P

coef_linear = 3.4445
coef_cubic = -4.775
coef_quintic = 2.0315
update_gain = 0.2 * math.sqrt(18432.0)

X, YL, Z, C, S = "x", "yl", "z", "c", "s"
NZ, NR = 8, 8
bf16, f32 = jnp.bfloat16, jnp.float32
COLS_Z = 768


def swap(a):
    return lax.ppermute(a, C, [(0, 1), (1, 0)])


def swap_slab(a):
    return lax.ppermute(a, S, [(0, 1), (1, 0)])


def shift_z(a, d):
    return lax.ppermute(a, Z, [((i + d) % NZ, i) for i in range(NZ)])


def turn(a):
    pairs = []
    for i in range(NZ):
        pairs += [(2 * ((i + 1) % NZ), 2 * i), (2 * ((i - 1) % NZ) + 1, 2 * i + 1)]
    return lax.ppermute(a, (Z, C), pairs)


def ring_z(a, b):
    mine, others = [a] + [None] * (NZ - 1), [b] + [None] * (NZ - 1)
    for step in range(1, 4):
        a = turn(a)
        b = turn(b)
        mine[step], others[step] = a, b
        mine[NZ - step], others[NZ - step] = swap(b), swap(a)
    mine[4] = turn(a)
    others[4] = swap(mine[4])
    return mine, others


def gather_r(a):
    copies = jnp.broadcast_to(a[None], (NR, *a.shape))
    return lax.all_to_all(copies, (X, YL), 0, 0, tiled=True)


def pick(a, index, axis):
    return lax.dynamic_index_in_dim(a, index, axis, keepdims=False)


def dot(a, b):
    return jnp.dot(a, b, preferred_element_type=f32)


def dot_t(a, b):
    return lax.dot_general(a, b, (((1,), (1,)), ((), ())), preferred_element_type=f32)


def t_dot(a, b):
    return lax.dot_general(a, b, (((0,), (0,)), ((), ())), preferred_element_type=f32)


ORDER = (0, 1, 7, 2, 6, 3, 5, 4)


def on_device(iterate):
    core, z = lax.axis_index(C), lax.axis_index(Z)
    first = core == 0
    up = 1 - 2 * core
    place = [(z + up * e + NZ) % NZ for e in range(NZ)]
    got = swap(iterate)
    top, low = jnp.where(first, iterate, got), jnp.where(first, got, iterate)
    chip = jnp.concatenate([top, low], axis=0).reshape(64, 2, 2304)
    mine, others = pick(chip, core, 1), pick(chip, 1 - core, 1)
    x_cols = gather_r(mine).reshape(NR, 2, 32, 2304)
    pieces = ring_z(mine, others)[0]
    x_rows = jnp.zeros((NZ, 64, 2304), bf16)
    for e in ORDER:
        x_rows = lax.dynamic_update_index_in_dim(x_rows, pieces[e], place[e], 0)
    x_rows = x_rows.reshape(512, 2304)
    cols_m = pick(x_cols, core, 1).reshape(256, 2304)
    cols_o = pick(x_cols, 1 - core, 1).reshape(256, 2304)

    other = dot_t(x_rows, cols_o).astype(bf16)
    own = dot_t(x_rows, cols_m) + swap(other).astype(f32)
    gram = (own + swap_slab(own.astype(bf16)).astype(f32)).astype(bf16)

    b_all = gather_r(gram).reshape(NR, NZ, 2, 32, 256)
    a_mine, a_others = ring_z(gram, swap(gram))
    squared = jnp.zeros((512, 256), f32)
    for e in ORDER:
        b = pick(b_all, place[e], 1)
        squared = squared + dot(a_mine[e], pick(b, core, 1).reshape(256, 256))
        squared = squared + dot(a_others[e], pick(b, 1 - core, 1).reshape(256, 256))
    poly_m = (coef_cubic * gram.astype(f32) + coef_quintic * squared).astype(bf16)
    poly_o = swap(poly_m)

    rest = x_rows[:, COLS_Z:]
    part_r = jnp.stack([t_dot(p, rest).astype(bf16).reshape(NR, 32, -1) for p in (poly_m, poly_o)], 1)
    got_r = lax.all_to_all(part_r, (X, YL), 0, 0, tiled=True)
    part_z = dot(poly_m, cols_m[:, :COLS_Z]) + dot(poly_o, cols_o[:, :COLS_Z])
    part_z = part_z.astype(bf16).reshape(NZ, 64, COLS_Z)
    take = lambda d: pick(part_z, (z - d + NZ) % NZ, 0)
    got_z = [shift_z(take(d), d) for d in (4, 1, 7, 2, 6, 3, 5)]
    sum_z = sum([p.astype(f32) for p in got_z], take(0).astype(f32)).reshape(2, 32, COLS_Z)
    sum_r = got_r.astype(f32).sum(0)

    def finish(half, k):
        applied = jnp.concatenate([pick(sum_z, half, 0), sum_r[k]], axis=1)
        stepped = coef_linear * pick(mine.reshape(2, 32, 2304), half, 0).astype(f32) + applied
        return (update_gain * stepped).astype(bf16)

    got = swap(finish(1 - core, 1))
    own = finish(core, 0)
    return jnp.concatenate([jnp.where(first, own, got), jnp.where(first, got, own)], axis=1)


def solution(mesh):
    fine = Mesh(mesh.devices.reshape(4, 2, 8, 2, 2), (X, YL, Z, C, S))
    spec = P((X, YL, Z, C), S)
    return jax.shard_map(on_device, mesh=fine, in_specs=(spec,), out_specs=spec, check_vma=False)
```

```python
import math

import jax
import jax.numpy as jnp
from jax import lax
from jax.experimental import pallas as pl
from jax.experimental.pallas import tpu as pltpu
from jax.sharding import Mesh
from jax.sharding import PartitionSpec as P

coef_linear = 3.4445
coef_cubic = -4.775
coef_quintic = 2.0315
update_gain = 0.2 * math.sqrt(18432.0)

X, YL, Z, C, S = "x", "yl", "z", "c", "s"
NZ, NR = 8, 8
ROWS, COLS = 32, 4608
TILE = 256
bf16, f32 = jnp.bfloat16, jnp.float32
ORDER = (0, 1, 7, 2, 6, 3, 5, 4)
PARTS = 16
K_PARTS = 2
OUT_PARTS = 9


def swap(a):
    return lax.ppermute(a, C, [(0, 1), (1, 0)])


def swap_slab(a):
    return lax.ppermute(a, S, [(0, 1), (1, 0)])


def turn(a):
    pairs = []
    for i in range(NZ):
        pairs += [(2 * ((i + 1) % NZ), 2 * i), (2 * ((i - 1) % NZ) + 1, 2 * i + 1)]
    return lax.ppermute(a, (Z, C), pairs)


def ring_z(a):
    b = swap(a)
    mine, others = [a] + [None] * (NZ - 1), [b] + [None] * (NZ - 1)
    for step in range(1, 4):
        a = turn(a)
        b = turn(b)
        mine[step], others[step] = a, b
        mine[NZ - step], others[NZ - step] = swap(b), swap(a)
    mine[4] = turn(a)
    others[4] = swap(mine[4])
    return [part[e] for e in ORDER for part in (mine, others)]


def where_from(i):
    core, z = lax.axis_index(C), lax.axis_index(Z)
    e = ORDER[i // 2]
    return (z + e + core * (NZ - 2 * e) + NZ) % NZ, core if i % 2 == 0 else 1 - core


def gather_r(a):
    copies = jnp.broadcast_to(a[None], (NR, *a.shape))
    return lax.all_to_all(copies, (X, YL), 0, 0, tiled=True)


def gram_kernel(*refs):
    pieces, (cols_ref, rows_ref, own_ref, sent_ref), (x, y, sem, sem_out) = refs[:PARTS], refs[PARTS:-4], refs[-4:]
    width = COLS // K_PARTS
    copies = []
    for k in range(K_PARTS):
        cut = pl.ds(k * width, width)
        group = [pltpu.make_async_copy(cols_ref.at[:, cut], y.at[:, cut], sem.at[k, PARTS])]
        for i, piece in enumerate(pieces):
            z, h = where_from(i)
            at = pl.ds(pl.multiple_of((2 * z + h) * ROWS, ROWS), ROWS)
            group.append(pltpu.make_async_copy(piece.at[:, cut], x.at[at, cut], sem.at[k, i]))
        for copy in group:
            copy.start()
        copies.append(group)
    total = None
    outs = []
    for k in range(K_PARTS):
        cut = pl.ds(k * width, width)
        for copy in copies[k]:
            copy.wait()
        out = pltpu.make_async_copy(x.at[:, cut], rows_ref.at[:, cut], sem_out.at[k])
        out.start()
        outs.append(out)
        term = lax.dot_general(x[:, cut], y[:, cut], (((1,), (1,)), ((), ())), preferred_element_type=f32)
        total = term if total is None else total + term
    own_ref[...] = total
    sent_ref[...] = total.astype(bf16)
    for out in outs:
        out.wait()


def gram_part(pieces, cols):
    n = 2 * NZ * ROWS
    return pl.pallas_call(
        gram_kernel,
        out_shape=(
            jax.ShapeDtypeStruct((n, COLS), bf16),
            jax.ShapeDtypeStruct((n, TILE), f32),
            jax.ShapeDtypeStruct((n, TILE), bf16),
        ),
        in_specs=[pl.BlockSpec(memory_space=pl.ANY)] * (PARTS + 1),
        out_specs=(
            pl.BlockSpec(memory_space=pl.ANY),
            pl.BlockSpec(memory_space=pltpu.VMEM),
            pl.BlockSpec(memory_space=pltpu.VMEM),
        ),
        scratch_shapes=[
            pltpu.VMEM((n, COLS), bf16),
            pltpu.VMEM((TILE, COLS), bf16),
            pltpu.SemaphoreType.DMA((K_PARTS, PARTS + 1)),
            pltpu.SemaphoreType.DMA((K_PARTS,)),
        ],
        compiler_params=pltpu.CompilerParams(vmem_limit_bytes=32 << 20),
        cost_estimate=pl.CostEstimate(flops=2 * n * TILE * COLS, bytes_accessed=12 << 20, transcendentals=0),
        name="gram_part",
    )(*pieces, cols)


def product_kernel(*refs):
    a_refs, (b_ref, rows_ref, out_ref), (a, b, x, out, sem_a, sem_b, sem_x, sem_out) = (
        refs[:PARTS],
        refs[PARTS:-8],
        refs[-8:],
    )
    copies = []
    for i, ref in enumerate(a_refs):
        z, h = where_from(i)
        copies.append(pltpu.make_async_copy(ref, a.at[:, pl.ds(i * TILE, TILE)], sem_a.at[i]))
        copies.append(pltpu.make_async_copy(b_ref.at[:, z, h], b.at[i], sem_b.at[i]))
    for copy in copies:
        copy.start()
    load = pltpu.make_async_copy(rows_ref, x, sem_x)
    load.start()
    for copy in copies:
        copy.wait()
    squared = jnp.dot(a[...], b[...].reshape(PARTS * TILE, TILE), preferred_element_type=f32)
    gram = a[:, pl.ds(0, TILE)].astype(f32)
    poly = (coef_cubic * gram + coef_quintic * squared).astype(bf16)
    load.wait()
    width = COLS // OUT_PARTS
    outs = []
    for k in range(OUT_PARTS):
        cut = pl.ds(k * width, width)
        term = lax.dot_general(poly, x[:, cut], (((0,), (0,)), ((), ())), preferred_element_type=f32)
        out[:, cut] = term.astype(bf16)
        copy = pltpu.make_async_copy(out.at[:, cut], out_ref.at[:, cut], sem_out.at[k])
        copy.start()
        outs.append(copy)
    for copy in outs:
        copy.wait()


def product_part(a_parts, b, rows):
    n = 2 * NZ * ROWS
    return pl.pallas_call(
        product_kernel,
        out_shape=jax.ShapeDtypeStruct((TILE, COLS), bf16),
        in_specs=[pl.BlockSpec(memory_space=pl.ANY)] * (PARTS + 2),
        out_specs=pl.BlockSpec(memory_space=pl.ANY),
        scratch_shapes=[
            pltpu.VMEM((n, PARTS * TILE), bf16),
            pltpu.VMEM((PARTS, NR, ROWS, TILE), bf16),
            pltpu.VMEM((n, COLS), bf16),
            pltpu.VMEM((TILE, COLS), bf16),
            pltpu.SemaphoreType.DMA((PARTS,)),
            pltpu.SemaphoreType.DMA((PARTS,)),
            pltpu.SemaphoreType.DMA,
            pltpu.SemaphoreType.DMA((OUT_PARTS,)),
        ],
        compiler_params=pltpu.CompilerParams(vmem_limit_bytes=32 << 20),
        cost_estimate=pl.CostEstimate(
            flops=2 * n * TILE * (COLS + PARTS * TILE), bytes_accessed=14 << 20, transcendentals=0
        ),
        name="product_part",
    )(*a_parts, b, rows)


def on_device(iterate):
    cols = gather_r(iterate).reshape(TILE, COLS)
    rows, own, sent = gram_part(ring_z(iterate), cols)
    gram = (own + swap_slab(sent).astype(f32)).astype(bf16)
    every = gather_r(gram).reshape(NR, NZ, 2, ROWS, TILE)
    part = product_part(ring_z(gram), every, rows)
    got = lax.all_to_all(part.reshape(NR, ROWS, COLS), (X, YL), 0, 0, tiled=True)
    stepped = coef_linear * iterate.astype(f32) + got.astype(f32).sum(0)
    return (update_gain * stepped).astype(bf16)


def solution(mesh):
    fine = Mesh(mesh.devices.reshape(4, 2, 8, 2, 2), (X, YL, Z, C, S))
    spec = P((X, YL, Z, C), S)
    return jax.shard_map(on_device, mesh=fine, in_specs=(spec,), out_specs=spec, check_vma=False)
```

```python
import math

import jax
import jax.numpy as jnp
from jax import lax
from jax.experimental import pallas as pl
from jax.experimental.pallas import tpu as pltpu
from jax.sharding import Mesh
from jax.sharding import PartitionSpec as P

coef_linear = 3.4445
coef_cubic = -4.775
coef_quintic = 2.0315
update_gain = 0.2 * math.sqrt(18432.0)

X, YL, Z, C, S = "x", "yl", "z", "c", "s"
NZ, NR = 8, 8
ROWS, COLS = 32, 4608
TILE = 256
bf16, f32 = jnp.bfloat16, jnp.float32
ORDER = (0, 1, 7, 2, 6, 3, 5, 4)
PARTS = 16
COLS_Z = 1536
LATE = 11
WIDTH = 512
GROUPS = 4
K_PARTS = 3
VMEM = pl.BlockSpec(memory_space=pltpu.VMEM)
HBM = pl.BlockSpec(memory_space=pltpu.HBM)


def swap(a):
    return lax.ppermute(a, C, [(0, 1), (1, 0)])


def swap_slab(a):
    return lax.ppermute(a, S, [(0, 1), (1, 0)])


def turn(a):
    pairs = []
    for i in range(NZ):
        pairs += [(2 * ((i + 1) % NZ), 2 * i), (2 * ((i - 1) % NZ) + 1, 2 * i + 1)]
    return lax.ppermute(a, (Z, C), pairs)


def far(a):
    return pltpu.with_memory_space_constraint(a, pltpu.HBM)


def ring_z(a, b=None):
    b = swap(a) if b is None else b
    mine, others = [a] + [None] * (NZ - 1), [b] + [None] * (NZ - 1)
    for step in range(1, 4):
        a = turn(a)
        b = turn(b)
        mine[step], others[step] = a, b
        mine[NZ - step], others[NZ - step] = swap(b), swap(a)
    mine[4] = turn(a)
    others[4] = swap(mine[4])
    return [part[e] for e in ORDER for part in (mine, others)]


def where_from(i):
    core, z = lax.axis_index(C), lax.axis_index(Z)
    e = ORDER[i // 2]
    return (z + e + core * (NZ - 2 * e) + NZ) % NZ, core if i % 2 == 0 else 1 - core


def near(a):
    return pltpu.with_memory_space_constraint(a, pltpu.VMEM)


def copies_kernel(a_ref, out_ref, sem):
    copies = [pltpu.make_async_copy(a_ref, out_ref.at[i], sem.at[i]) for i in range(NR)]
    for copy in copies:
        copy.start()
    for copy in copies:
        copy.wait()


def gather_r(a):
    copies = pl.pallas_call(
        copies_kernel,
        out_shape=pltpu.HBM((NR, *a.shape), a.dtype),
        in_specs=[VMEM],
        out_specs=HBM,
        scratch_shapes=[pltpu.SemaphoreType.DMA((NR,))],
        compiler_params=pltpu.CompilerParams(vmem_limit_bytes=1 << 20),
        name="copies",
    )(near(a))
    return lax.all_to_all(copies, (X, YL), 0, 0, tiled=True)


def gram_kernel(*refs):
    pieces, (cols_ref, rows_ref, cut_ref, own_ref, sent_ref, x, sem, sem_out) = refs[:PARTS], refs[PARTS:]
    width = COLS // K_PARTS
    cuts = [pl.ds(k * width, width) for k in range(K_PARTS)]
    copies = []
    for k, cut in enumerate(cuts):
        for i, piece in enumerate(pieces):
            z, h = where_from(i)
            copies.append(pltpu.make_async_copy(piece.at[:, cut], x.at[2 * z + h, :, cut], sem.at[k, i]))
            copies[-1].start()
    outs = [pltpu.make_async_copy(cols_ref.at[:, :, pl.ds(0, COLS_Z)], cut_ref, sem_out.at[K_PARTS])]
    outs[0].start()
    total = None
    for k, cut in enumerate(cuts):
        for copy in copies[k * PARTS : (k + 1) * PARTS]:
            copy.wait()
        outs.append(pltpu.make_async_copy(x.at[:, :, cut], rows_ref.at[:, :, cut], sem_out.at[k]))
        outs[-1].start()
        left = x[:, :, cut].reshape(PARTS * ROWS, width)
        right = cols_ref[:, :, cut].reshape(TILE, width)
        term = lax.dot_general(left, right, (((1,), (1,)), ((), ())), preferred_element_type=f32)
        total = term if total is None else total + term
    own_ref[...] = total
    sent_ref[...] = total.astype(bf16)
    for out in outs:
        out.wait()


def gram_part(pieces, cols):
    n = PARTS * ROWS
    return pl.pallas_call(
        gram_kernel,
        out_shape=(
            pltpu.HBM((PARTS, ROWS, COLS), bf16),
            pltpu.HBM((NR, ROWS, COLS_Z), bf16),
            pltpu.VMEM((n, TILE), f32),
            pltpu.VMEM((n, TILE), bf16),
        ),
        in_specs=[HBM] * LATE + [VMEM] * (PARTS - LATE) + [VMEM],
        out_specs=(HBM, HBM, VMEM, VMEM),
        scratch_shapes=[
            pltpu.VMEM((PARTS, ROWS, COLS), bf16),
            pltpu.SemaphoreType.DMA((K_PARTS, PARTS)),
            pltpu.SemaphoreType.DMA((K_PARTS + 1,)),
        ],
        compiler_params=pltpu.CompilerParams(vmem_limit_bytes=12 << 20),
        cost_estimate=pl.CostEstimate(flops=2 * n * TILE * COLS, bytes_accessed=12 << 20, transcendentals=0),
        name="gram_part",
    )(*[far(p) for p in pieces[:LATE]], *[near(p) for p in pieces[LATE:]], near(cols))


def product_kernel(*refs):
    a_refs, refs = refs[:PARTS], refs[PARTS:]
    b_ref, rows_ref, cut_ref, out_ref, own_ref, other_ref, a, b, x, y, part, out, sem_a, sem_b, sem_x, sem_out = refs
    copies = []
    for i, ref in enumerate(a_refs):
        z, h = where_from(i)
        copies.append(pltpu.make_async_copy(ref, a.at[:, pl.ds(i * TILE, TILE)], sem_a.at[i]))
        copies.append(pltpu.make_async_copy(b_ref.at[:, 2 * z + h], b.at[i], sem_b.at[i]))
    loads = [pltpu.make_async_copy(cut_ref, y, sem_x.at[0]), pltpu.make_async_copy(rows_ref, x, sem_x.at[1])]
    for copy in copies + loads:
        copy.start()
    squared = None
    size = PARTS // GROUPS
    for g in range(GROUPS):
        for copy in copies[2 * g * size : 2 * (g + 1) * size]:
            copy.wait()
        left = a[:, pl.ds(g * size * TILE, size * TILE)]
        right = b[pl.ds(g * size, size)].reshape(size * TILE, TILE)
        term = jnp.dot(left, right, preferred_element_type=f32)
        squared = term if squared is None else squared + term
    gram = a[:, pl.ds(0, TILE)].astype(f32)
    poly = (coef_cubic * gram + coef_quintic * squared).astype(bf16)
    loads[0].wait()
    for k in range(COLS_Z // WIDTH):
        cut = pl.ds(k * WIDTH, WIDTH)
        term = jnp.dot(poly, y[:, :, cut].reshape(TILE, WIDTH), preferred_element_type=f32)
        part[:, :, :, cut] = term.astype(bf16).reshape(NZ, 2, ROWS, WIDTH)
    core = lax.axis_index(C)
    outs = [
        pltpu.make_async_copy(part.at[:, 1 - core], other_ref, sem_x.at[0]),
        pltpu.make_async_copy(part.at[:, core], own_ref, sem_x.at[2]),
    ]
    for copy in outs:
        copy.start()
    loads[1].wait()
    for k in range((COLS - COLS_Z) // WIDTH):
        cut = pl.ds(k * WIDTH, WIDTH)
        right = x[:, :, pl.ds(COLS_Z + k * WIDTH, WIDTH)].reshape(PARTS * ROWS, WIDTH)
        term = lax.dot_general(poly, right, (((0,), (0,)), ((), ())), preferred_element_type=f32)
        out[:, :, cut] = term.astype(bf16).reshape(NR, ROWS, WIDTH)
        outs.append(pltpu.make_async_copy(out.at[:, :, cut], out_ref.at[:, :, cut], sem_out.at[k]))
        outs[-1].start()
    for copy in outs:
        copy.wait()


def product_part(a_parts, b, rows, cut):
    n = PARTS * ROWS
    return pl.pallas_call(
        product_kernel,
        out_shape=(
            pltpu.HBM((NR, ROWS, COLS - COLS_Z), bf16),
            pltpu.HBM((NZ, ROWS, COLS_Z), bf16),
            pltpu.HBM((NZ, ROWS, COLS_Z), bf16),
        ),
        in_specs=[HBM] * LATE + [VMEM] * (PARTS - LATE) + [VMEM, HBM, HBM],
        out_specs=(HBM, HBM, HBM),
        scratch_shapes=[
            pltpu.VMEM((n, PARTS * TILE), bf16),
            pltpu.VMEM((PARTS, NR, ROWS, TILE), bf16),
            pltpu.VMEM((PARTS, ROWS, COLS), bf16),
            pltpu.VMEM((NR, ROWS, COLS_Z), bf16),
            pltpu.VMEM((NZ, 2, ROWS, COLS_Z), bf16),
            pltpu.VMEM((NR, ROWS, COLS - COLS_Z), bf16),
            pltpu.SemaphoreType.DMA((PARTS,)),
            pltpu.SemaphoreType.DMA((PARTS,)),
            pltpu.SemaphoreType.DMA((3,)),
            pltpu.SemaphoreType.DMA(((COLS - COLS_Z) // WIDTH,)),
        ],
        compiler_params=pltpu.CompilerParams(vmem_limit_bytes=28 << 20),
        cost_estimate=pl.CostEstimate(
            flops=2 * n * TILE * (COLS + PARTS * TILE), bytes_accessed=14 << 20, transcendentals=0
        ),
        name="product_part",
    )(*[far(p) for p in a_parts[:LATE]], *[near(p) for p in a_parts[LATE:]], near(b), far(rows), far(cut))


def shift_z(a, d):
    return lax.ppermute(a, Z, [((i + d) % NZ, i) for i in range(NZ)])


def on_device(iterate):
    z = lax.axis_index(Z)
    cols = gather_r(iterate)
    rows, cut, own, sent = gram_part(ring_z(iterate), cols)
    gram = (own + swap_slab(sent).astype(f32)).astype(bf16)
    mine, twin = lax.optimization_barrier((gram, swap(gram)))
    a_parts = ring_z(gram, twin)
    every = gather_r(mine).reshape(NR, PARTS, ROWS, TILE)
    parts, own, other = product_part(a_parts, every, rows, cut)
    got = lax.all_to_all(parts, (X, YL), 0, 0, tiled=True)
    own = (own.astype(f32) + swap(other).astype(f32)).astype(bf16)
    take = lambda d: lax.dynamic_index_in_dim(own, (z - d + NZ) % NZ, 0, keepdims=False)
    got_z = [take(0)] + [shift_z(take(d), d) for d in (4, 1, 7, 2, 6, 3, 5)]
    sums = [sum(p.astype(f32) for p in got_z), got.astype(f32).sum(0)]
    total = coef_linear * iterate.astype(f32) + jnp.concatenate(sums, axis=1)
    return (update_gain * total).astype(bf16)


def solution(mesh):
    fine = Mesh(mesh.devices.reshape(4, 2, 8, 2, 2), (X, YL, Z, C, S))
    spec = P((X, YL, Z, C), S)
    return jax.shard_map(on_device, mesh=fine, in_specs=(spec,), out_specs=spec, check_vma=False)
```

```python
import functools
import math

import jax
import jax.numpy as jnp
from jax import lax
from jax.experimental import pallas as pl
from jax.experimental.pallas import tpu as pltpu
from jax.sharding import Mesh
from jax.sharding import PartitionSpec as P

coef_linear = 3.4445
coef_cubic = -4.775
coef_quintic = 2.0315
update_gain = 0.2 * math.sqrt(18432.0)

X, YL, Z, C, S = "x", "yl", "z", "c", "s"
NZ, NR = 8, 8
ROWS, COLS = 32, 4608
TILE = 256
bf16, f32 = jnp.bfloat16, jnp.float32
ORDER = (0, 1, 7, 2, 6, 3, 5, 4)
PARTS = 16
COLS_Z = 1280
LATE = 11
EARLY = 12
NEAR = 0
WIDTH_Z, WIDTH = 640, 256
VMEM = pl.BlockSpec(memory_space=pltpu.VMEM)
HBM = pl.BlockSpec(memory_space=pltpu.HBM)


def swap(a):
    return lax.ppermute(a, C, [(0, 1), (1, 0)])


def swap_slab(a):
    return lax.ppermute(a, S, [(0, 1), (1, 0)])


def turn(a):
    pairs = []
    for i in range(NZ):
        pairs += [(2 * ((i + 1) % NZ), 2 * i), (2 * ((i - 1) % NZ) + 1, 2 * i + 1)]
    return lax.ppermute(a, (Z, C), pairs)


def far(a):
    return pltpu.with_memory_space_constraint(a, pltpu.HBM)


def ring_z(a, b):
    mine, others = [a] + [None] * (NZ - 1), [b] + [None] * (NZ - 1)
    for step in range(1, 4):
        a = turn(a)
        b = turn(b)
        mine[step], others[step] = a, b
        mine[NZ - step], others[NZ - step] = swap(b), swap(a)
    mine[4] = turn(a)
    others[4] = swap(mine[4])
    return [part[e] for e in ORDER for part in (mine, others)]


def where_from(i):
    core, z = lax.axis_index(C), lax.axis_index(Z)
    e = ORDER[i // 2]
    return (z + e + core * (NZ - 2 * e) + NZ) % NZ, core if i % 2 == 0 else 1 - core


def near(a):
    return pltpu.with_memory_space_constraint(a, pltpu.VMEM)


def spread(a_ref, out_ref, sem):
    copies = [pltpu.make_async_copy(a_ref, out_ref.at[i], sem.at[i]) for i in range(NR)]
    for copy in copies:
        copy.start()
    for copy in copies:
        copy.wait()


def copies_of(a):
    return pl.pallas_call(
        spread,
        out_shape=pltpu.HBM((NR, *a.shape), a.dtype),
        in_specs=[VMEM],
        out_specs=HBM,
        scratch_shapes=[pltpu.SemaphoreType.DMA((NR,))],
        compiler_params=pltpu.CompilerParams(vmem_limit_bytes=1 << 20),
        cost_estimate=pl.CostEstimate(flops=0, bytes_accessed=5 << 20, transcendentals=0),
        name="copies",
    )(near(a))


def gather_r(copies):
    return lax.all_to_all(copies, (X, YL), 0, 0, tiled=True)


def join_kernel(own_a, got_a, own_b, got_b, gram_ref):
    for i in range(PARTS):
        z, h = where_from(i)
        if i < EARLY:
            rows = pl.ds(i * ROWS, ROWS)
            value = own_a[rows, :] + got_a[rows, :].astype(f32)
        else:
            rows = pl.ds((i - EARLY) * ROWS, ROWS)
            value = own_b[rows, :] + got_b[rows, :].astype(f32)
        gram_ref[2 * z + h] = value.astype(bf16)


def join(*parts):
    return pl.pallas_call(
        join_kernel,
        out_shape=pltpu.VMEM((PARTS, ROWS, TILE), bf16),
        in_specs=[VMEM] * 4,
        out_specs=VMEM,
        compiler_params=pltpu.CompilerParams(vmem_limit_bytes=4 << 20),
        name="join",
    )(*[near(p) for p in parts])


def gram_kernel(count, cut, *refs):
    pieces, cols_ref, own_ref, sent_ref = refs[:count], refs[count], refs[count + 1], refs[count + 2]
    x, sem = refs[-2:]
    copies = [pltpu.make_async_copy(piece, x.at[i], sem.at[i]) for i, piece in enumerate(pieces)]
    if cut:
        copies.append(pltpu.make_async_copy(cols_ref.at[:, :, pl.ds(0, COLS_Z)], refs[count + 3], sem.at[count]))
    for copy in copies:
        copy.start()
    for copy in copies[:count]:
        copy.wait()
    left = x[...].reshape(count * ROWS, COLS)
    right = cols_ref[...].reshape(TILE, COLS)
    total = lax.dot_general(left, right, (((1,), (1,)), ((), ())), preferred_element_type=f32)
    own_ref[...] = total
    sent_ref[...] = total.astype(bf16)
    for copy in copies[count:]:
        copy.wait()


def gram_part(pieces, near_from, cols, cut):
    count = len(pieces)
    n = count * ROWS
    outs = [pltpu.VMEM((n, TILE), f32), pltpu.VMEM((n, TILE), bf16)]
    if cut:
        outs.append(pltpu.HBM((NR, ROWS, COLS_Z), bf16))
    return pl.pallas_call(
        functools.partial(gram_kernel, count, cut),
        out_shape=tuple(outs),
        in_specs=[HBM] * near_from + [VMEM] * (count - near_from) + [VMEM],
        out_specs=(VMEM, VMEM, HBM)[: len(outs)],
        scratch_shapes=[
            pltpu.VMEM((count, ROWS, COLS), bf16),
            pltpu.SemaphoreType.DMA((count + 1,)),
        ],
        compiler_params=pltpu.CompilerParams(vmem_limit_bytes=10 << 20),
        cost_estimate=pl.CostEstimate(flops=2 * n * TILE * COLS, bytes_accessed=6 << 20, transcendentals=0),
        name="gram_part",
    )(*[far(p) for p in pieces[:near_from]], *[near(p) for p in pieces[near_from:]], near(cols))


def product_kernel(*refs):
    a_refs, refs = refs[:PARTS], refs[PARTS:]
    x_refs, refs = refs[:PARTS], refs[PARTS:]
    b_ref, cut_ref, out_ref, own_ref, other_ref, a, x, y, part, out, sem_a, sem_x, sem_out = refs
    copies = []
    for i, ref in enumerate(a_refs):
        z, h = where_from(i)
        copies.append(pltpu.make_async_copy(ref, a.at[i], sem_a.at[i]))
    loads = [pltpu.make_async_copy(cut_ref, y, sem_x.at[PARTS])]
    for i, ref in enumerate(x_refs):
        z, h = where_from(i)
        loads.append(pltpu.make_async_copy(ref.at[:, pl.ds(COLS_Z, COLS - COLS_Z)], x.at[2 * z + h], sem_x.at[i]))
    for copy in copies + loads:
        copy.start()
    squared = None
    for i in range(PARTS):
        z, h = where_from(i)
        copies[i].wait()
        term = jnp.dot(a[i], b_ref[:, 2 * z + h].reshape(TILE, TILE), preferred_element_type=f32)
        squared = term if squared is None else squared + term
    gram = a[0].astype(f32)
    poly = coef_cubic * gram + coef_quintic * squared
    poly_t = poly.T.astype(bf16)
    poly = poly.astype(bf16)
    loads[0].wait()
    for k in range(COLS_Z // WIDTH_Z):
        cut = pl.ds(k * WIDTH_Z, WIDTH_Z)
        term = jnp.dot(poly, y[:, :, cut].reshape(TILE, WIDTH_Z), preferred_element_type=f32)
        part[:, :, :, cut] = term.astype(bf16).reshape(NZ, 2, ROWS, WIDTH_Z)
    core = lax.axis_index(C)
    outs = [
        pltpu.make_async_copy(part.at[:, 1 - core], other_ref, sem_x.at[PARTS + 1]),
        pltpu.make_async_copy(part.at[:, core], own_ref, sem_x.at[PARTS + 2]),
    ]
    for copy in outs:
        copy.start()
    for load in loads[1:]:
        load.wait()
    for k in range((COLS - COLS_Z) // WIDTH):
        cut = pl.ds(k * WIDTH, WIDTH)
        right = x[:, :, cut].reshape(PARTS * ROWS, WIDTH)
        term = jnp.dot(poly_t, right, preferred_element_type=f32)
        out[:, :, cut] = term.astype(bf16).reshape(NR, ROWS, WIDTH)
        outs.append(pltpu.make_async_copy(out.at[:, :, cut], out_ref.at[:, :, cut], sem_out.at[k]))
        outs[-1].start()
    for copy in outs:
        copy.wait()


def product_part(a_parts, x_parts, b, cut):
    n = PARTS * ROWS
    return pl.pallas_call(
        product_kernel,
        out_shape=(
            pltpu.HBM((NR, ROWS, COLS - COLS_Z), bf16),
            pltpu.HBM((NZ, ROWS, COLS_Z), bf16),
            pltpu.HBM((NZ, ROWS, COLS_Z), bf16),
        ),
        in_specs=[HBM] * LATE + [VMEM] * (PARTS - LATE) + [HBM] * PARTS + [VMEM, HBM],
        out_specs=(HBM, HBM, HBM),
        scratch_shapes=[
            pltpu.VMEM((PARTS, n, TILE), bf16),
            pltpu.VMEM((PARTS, ROWS, COLS - COLS_Z), bf16),
            pltpu.VMEM((NR, ROWS, COLS_Z), bf16),
            pltpu.VMEM((NZ, 2, ROWS, COLS_Z), bf16),
            pltpu.VMEM((NR, ROWS, COLS - COLS_Z), bf16),
            pltpu.SemaphoreType.DMA((PARTS,)),
            pltpu.SemaphoreType.DMA((PARTS + 3,)),
            pltpu.SemaphoreType.DMA(((COLS - COLS_Z) // WIDTH,)),
        ],
        compiler_params=pltpu.CompilerParams(vmem_limit_bytes=28 << 20),
        cost_estimate=pl.CostEstimate(
            flops=2 * n * TILE * (COLS + PARTS * TILE), bytes_accessed=14 << 20, transcendentals=0
        ),
        name="product_part",
    )(*[far(p) for p in a_parts[:LATE]], *[near(p) for p in a_parts[LATE:]], *[far(p) for p in x_parts], near(b), far(cut))


def shift_z(a, d):
    return lax.ppermute(a, Z, [((i + d) % NZ, i) for i in range(NZ)])


def on_device(iterate):
    z = lax.axis_index(Z)
    copies, twin = lax.optimization_barrier((copies_of(iterate), swap(iterate)))
    cols = gather_r(copies)
    pieces = ring_z(iterate, twin)
    own_a, sent_a, cut = gram_part(pieces[:EARLY], EARLY, cols, True)
    got_a = swap_slab(sent_a)
    own_b, sent_b = gram_part(pieces[EARLY:], NEAR, cols, False)
    gram = join(own_a, got_a, own_b, swap_slab(sent_b))
    gram = gram.reshape(PARTS * ROWS, TILE)
    copies, twin = lax.optimization_barrier((copies_of(gram), swap(gram)))
    every = gather_r(copies).reshape(NR, PARTS, ROWS, TILE)
    parts, own, other = product_part(ring_z(gram, twin), pieces, every, cut)
    got = lax.all_to_all(parts, (X, YL), 0, 0, tiled=True)
    own = (own.astype(f32) + swap(other).astype(f32)).astype(bf16)
    take = lambda d: lax.dynamic_index_in_dim(own, (z - d + NZ) % NZ, 0, keepdims=False)
    got_z = [take(0)] + [shift_z(take(d), d) for d in (4, 1, 7, 2, 6, 3, 5)]
    sums = [sum(p.astype(f32) for p in got_z), got.astype(f32).sum(0)]
    total = coef_linear * iterate.astype(f32) + jnp.concatenate(sums, axis=1)
    return (update_gain * total).astype(bf16)


def solution(mesh):
    fine = Mesh(mesh.devices.reshape(4, 2, 8, 2, 2), (X, YL, Z, C, S))
    spec = P((X, YL, Z, C), S)
    return jax.shard_map(on_device, mesh=fine, in_specs=(spec,), out_specs=spec, check_vma=False)
```

```python
import functools
import math

import jax
import jax.numpy as jnp
from jax import lax
from jax.experimental import pallas as pl
from jax.experimental.pallas import tpu as pltpu
from jax.sharding import Mesh
from jax.sharding import PartitionSpec as P

coef_linear = 3.4445
coef_cubic = -4.775
coef_quintic = 2.0315
update_gain = 0.2 * math.sqrt(18432.0)

X, YL, Z, C, S = "x", "yl", "z", "c", "s"
NZ, NR = 8, 8
ROWS, COLS = 32, 4608
TILE = 256
bf16, f32 = jnp.bfloat16, jnp.float32
ORDER = (0, 1, 7, 2, 6, 3, 5, 4)
PARTS = 16
COLS_Z = 1536
LATE = 11
EARLY = 12
NEAR = 0
WIDTH_Z, WIDTH = 512, 256
SINGLE = {4: 6, 0: 7}
VMEM = pl.BlockSpec(memory_space=pltpu.VMEM)
HBM = pl.BlockSpec(memory_space=pltpu.HBM)


def swap(a):
    return lax.ppermute(a, C, [(0, 1), (1, 0)])


def swap_slab(a):
    return lax.ppermute(a, S, [(0, 1), (1, 0)])


def turn(a):
    pairs = []
    for i in range(NZ):
        pairs += [(2 * ((i + 1) % NZ), 2 * i), (2 * ((i - 1) % NZ) + 1, 2 * i + 1)]
    return lax.ppermute(a, (Z, C), pairs)


def far(a):
    return pltpu.with_memory_space_constraint(a, pltpu.HBM)


def ring_z(a, b):
    mine, others = [a] + [None] * (NZ - 1), [b] + [None] * (NZ - 1)
    for step in range(1, 4):
        a = turn(a)
        b = turn(b)
        mine[step], others[step] = a, b
        mine[NZ - step], others[NZ - step] = swap(b), swap(a)
    mine[4] = turn(a)
    others[4] = swap(mine[4])
    return [part[e] for e in ORDER for part in (mine, others)]


def where_from(i):
    core, z = lax.axis_index(C), lax.axis_index(Z)
    e = ORDER[i // 2]
    return (z + e + core * (NZ - 2 * e) + NZ) % NZ, core if i % 2 == 0 else 1 - core


def near(a):
    return pltpu.with_memory_space_constraint(a, pltpu.VMEM)


def spread(a_ref, out_ref, sem):
    copies = [pltpu.make_async_copy(a_ref, out_ref.at[i], sem.at[i]) for i in range(NR)]
    for copy in copies:
        copy.start()
    for copy in copies:
        copy.wait()


def copies_of(a):
    return pl.pallas_call(
        spread,
        out_shape=pltpu.HBM((NR, *a.shape), a.dtype),
        in_specs=[VMEM],
        out_specs=HBM,
        scratch_shapes=[pltpu.SemaphoreType.DMA((NR,))],
        compiler_params=pltpu.CompilerParams(vmem_limit_bytes=1 << 20),
        cost_estimate=pl.CostEstimate(flops=0, bytes_accessed=5 << 20, transcendentals=0),
        name="copies",
    )(near(a))


def gather_r(copies):
    return lax.all_to_all(copies, (X, YL), 0, 0, tiled=True)


def join_kernel(own_a, got_a, own_b, got_b, gram_ref):
    for i in range(PARTS):
        z, h = where_from(i)
        if i < EARLY:
            rows = pl.ds(i * ROWS, ROWS)
            value = own_a[rows, :] + got_a[rows, :].astype(f32)
        else:
            rows = pl.ds((i - EARLY) * ROWS, ROWS)
            value = own_b[rows, :] + got_b[rows, :].astype(f32)
        gram_ref[2 * z + h] = value.astype(bf16)


def join(*parts):
    return pl.pallas_call(
        join_kernel,
        out_shape=pltpu.VMEM((PARTS, ROWS, TILE), bf16),
        in_specs=[VMEM] * 4,
        out_specs=VMEM,
        compiler_params=pltpu.CompilerParams(vmem_limit_bytes=4 << 20),
        name="join",
    )(*[near(p) for p in parts])


def gram_kernel(count, cut, *refs):
    pieces, cols_ref, own_ref, sent_ref = refs[:count], refs[count], refs[count + 1], refs[count + 2]
    x, sem = refs[-2:]
    copies = [pltpu.make_async_copy(piece, x.at[i], sem.at[i]) for i, piece in enumerate(pieces)]
    if cut:
        copies.append(pltpu.make_async_copy(cols_ref.at[:, :, pl.ds(0, COLS_Z)], refs[count + 3], sem.at[count]))
    for copy in copies:
        copy.start()
    for copy in copies[:count]:
        copy.wait()
    left = x[...].reshape(count * ROWS, COLS)
    right = cols_ref[...].reshape(TILE, COLS)
    total = lax.dot_general(left, right, (((1,), (1,)), ((), ())), preferred_element_type=f32)
    own_ref[...] = total
    sent_ref[...] = total.astype(bf16)
    for copy in copies[count:]:
        copy.wait()


def gram_part(pieces, near_from, cols, cut):
    count = len(pieces)
    n = count * ROWS
    outs = [pltpu.VMEM((n, TILE), f32), pltpu.VMEM((n, TILE), bf16)]
    if cut:
        outs.append(pltpu.HBM((NR, ROWS, COLS_Z), bf16))
    return pl.pallas_call(
        functools.partial(gram_kernel, count, cut),
        out_shape=tuple(outs),
        in_specs=[HBM] * near_from + [VMEM] * (count - near_from) + [VMEM],
        out_specs=(VMEM, VMEM, HBM)[: len(outs)],
        scratch_shapes=[
            pltpu.VMEM((count, ROWS, COLS), bf16),
            pltpu.SemaphoreType.DMA((count + 1,)),
        ],
        compiler_params=pltpu.CompilerParams(vmem_limit_bytes=10 << 20),
        cost_estimate=pl.CostEstimate(flops=2 * n * TILE * COLS, bytes_accessed=6 << 20, transcendentals=0),
        name="gram_part",
    )(*[far(p) for p in pieces[:near_from]], *[near(p) for p in pieces[near_from:]], near(cols))


def product_kernel(*refs):
    a_refs, refs = refs[:PARTS], refs[PARTS:]
    x_refs, refs = refs[:PARTS], refs[PARTS:]
    b_ref, cut_ref, out_ref, own_ref, other_ref, a, x, y, part, out, sem_a, sem_x, sem_out = refs
    copies = []
    for i, ref in enumerate(a_refs):
        z, h = where_from(i)
        copies.append(pltpu.make_async_copy(ref, a.at[i], sem_a.at[i]))
    loads = [pltpu.make_async_copy(cut_ref, y, sem_x.at[PARTS])]
    for i, ref in enumerate(x_refs):
        z, h = where_from(i)
        loads.append(pltpu.make_async_copy(ref.at[:, pl.ds(COLS_Z, COLS - COLS_Z)], x.at[2 * z + h], sem_x.at[i]))
    for copy in copies + loads:
        copy.start()
    squared = None
    for i in range(PARTS):
        z, h = where_from(i)
        copies[i].wait()
        term = jnp.dot(a[i], b_ref[:, 2 * z + h].reshape(TILE, TILE), preferred_element_type=f32)
        squared = term if squared is None else squared + term
    gram = a[0].astype(f32)
    poly = coef_cubic * gram + coef_quintic * squared
    poly_t = poly.T.astype(bf16)
    poly = poly.astype(bf16)
    loads[0].wait()
    for k in range(COLS_Z // WIDTH_Z):
        cut = pl.ds(k * WIDTH_Z, WIDTH_Z)
        term = jnp.dot(poly, y[:, :, cut].reshape(TILE, WIDTH_Z), preferred_element_type=f32)
        part[:, :, :, cut] = term.astype(bf16).reshape(NZ, 2, ROWS, WIDTH_Z)
    core, z = lax.axis_index(C), lax.axis_index(Z)
    outs = []
    for e in range(5):
        for ref, c in ((other_ref, 1 - core), (own_ref, core)):
            at = (z + e + c * (NZ - 2 * e)) % NZ
            if e in (0, 4):
                block = (part.at[at, c], ref.at[SINGLE[e]])
            else:
                block = (part.at[at], ref.at[pl.ds(2 * e - 2, 2)])
            outs.append(pltpu.make_async_copy(*block, sem_x.at[PARTS + 1 + len(outs)]))
    for copy in outs:
        copy.start()
    for load in loads[1:]:
        load.wait()
    for k in range((COLS - COLS_Z) // WIDTH):
        cut = pl.ds(k * WIDTH, WIDTH)
        right = x[:, :, cut].reshape(PARTS * ROWS, WIDTH)
        term = jnp.dot(poly_t, right, preferred_element_type=f32)
        out[:, :, cut] = term.astype(bf16).reshape(NR, ROWS, WIDTH)
        outs.append(pltpu.make_async_copy(out.at[:, :, cut], out_ref.at[:, :, cut], sem_out.at[k]))
        outs[-1].start()
    for copy in outs:
        copy.wait()


def product_part(a_parts, x_parts, b, cut):
    n = PARTS * ROWS
    return pl.pallas_call(
        product_kernel,
        out_shape=(
            pltpu.HBM((NR, ROWS, COLS - COLS_Z), bf16),
            pltpu.HBM((NZ, ROWS, COLS_Z), bf16),
            pltpu.HBM((NZ, ROWS, COLS_Z), bf16),
        ),
        in_specs=[HBM] * LATE + [VMEM] * (PARTS - LATE) + [HBM] * PARTS + [VMEM, HBM],
        out_specs=(HBM, HBM, HBM),
        scratch_shapes=[
            pltpu.VMEM((PARTS, n, TILE), bf16),
            pltpu.VMEM((PARTS, ROWS, COLS - COLS_Z), bf16),
            pltpu.VMEM((NR, ROWS, COLS_Z), bf16),
            pltpu.VMEM((NZ, 2, ROWS, COLS_Z), bf16),
            pltpu.VMEM((NR, ROWS, COLS - COLS_Z), bf16),
            pltpu.SemaphoreType.DMA((PARTS,)),
            pltpu.SemaphoreType.DMA((PARTS + 11,)),
            pltpu.SemaphoreType.DMA(((COLS - COLS_Z) // WIDTH,)),
        ],
        compiler_params=pltpu.CompilerParams(vmem_limit_bytes=28 << 20),
        cost_estimate=pl.CostEstimate(
            flops=2 * n * TILE * (COLS + PARTS * TILE), bytes_accessed=14 << 20, transcendentals=0
        ),
        name="product_part",
    )(*[far(p) for p in a_parts[:LATE]], *[near(p) for p in a_parts[LATE:]], *[far(p) for p in x_parts], near(b), far(cut))


def cast(a, e):
    pairs = []
    for i in range(NZ):
        pairs += [(2 * ((i - e) % NZ), 2 * i), (2 * ((i + e) % NZ) + 1, 2 * i + 1)]
    return lax.ppermute(a, (Z, C), pairs)


def on_device(iterate):
    core = lax.axis_index(C)
    copies, twin = lax.optimization_barrier((copies_of(iterate), swap(iterate)))
    cols = gather_r(copies)
    pieces = ring_z(iterate, twin)
    own_a, sent_a, cut = gram_part(pieces[:EARLY], EARLY, cols, True)
    got_a = swap_slab(sent_a)
    own_b, sent_b = gram_part(pieces[EARLY:], NEAR, cols, False)
    gram = join(own_a, got_a, own_b, swap_slab(sent_b))
    gram = gram.reshape(PARTS * ROWS, TILE)
    copies, twin = lax.optimization_barrier((copies_of(gram), swap(gram)))
    every = gather_r(copies).reshape(NR, PARTS, ROWS, TILE)
    parts, own, other = product_part(ring_z(gram, twin), pieces, every, cut)
    got = lax.all_to_all(parts, (X, YL), 0, 0, tiled=True)
    own = (own.astype(f32) + swap(other).astype(f32)).astype(bf16)
    last = cast(own[6], 4)
    pairs = [cast(own[2 * e - 2 : 2 * e], e) for e in (3, 2, 1)]
    both = sum(p.astype(f32) for p in pairs)
    here = jnp.where(core == 0, both[0], both[1])
    there = jnp.where(core == 0, both[1], both[0]).astype(bf16)
    sum_z = here + last.astype(f32) + own[7].astype(f32) + swap(there).astype(f32)
    sum_r = got.astype(f32).sum(0)
    total = coef_linear * iterate.astype(f32) + jnp.concatenate([sum_z, sum_r], axis=1)
    return (update_gain * total).astype(bf16)


def solution(mesh):
    fine = Mesh(mesh.devices.reshape(4, 2, 8, 2, 2), (X, YL, Z, C, S))
    spec = P((X, YL, Z, C), S)
    return jax.shard_map(on_device, mesh=fine, in_specs=(spec,), out_specs=spec, check_vma=False)
```

```python
import functools
import math

import jax
import jax.numpy as jnp
from jax import lax
from jax.experimental import pallas as pl
from jax.experimental.pallas import tpu as pltpu
from jax.sharding import Mesh
from jax.sharding import PartitionSpec as P

coef_linear = 3.4445
coef_cubic = -4.775
coef_quintic = 2.0315
update_gain = 0.2 * math.sqrt(18432.0)

X, YL, Z, C, S = "x", "yl", "z", "c", "s"
NZ, NR = 8, 8
ROWS, COLS = 32, 4608
TILE = 256
bf16, f32 = jnp.bfloat16, jnp.float32
ORDER = (0, 1, 7, 2, 6, 3, 5, 4)
PARTS = 16
COLS_Z = 1536
LATE = 11
EARLY = 12
NEAR = 0
WIDTH_Z, WIDTH = 768, 768
SINGLE = {4: 6, 0: 7}
TOGETHER = 2
VMEM = pl.BlockSpec(memory_space=pltpu.VMEM)
HBM = pl.BlockSpec(memory_space=pltpu.HBM)


def swap(a):
    return lax.ppermute(a, C, [(0, 1), (1, 0)])


def swap_slab(a):
    return lax.ppermute(a, S, [(0, 1), (1, 0)])


def turn(a):
    pairs = []
    for i in range(NZ):
        pairs += [(2 * ((i + 1) % NZ), 2 * i), (2 * ((i - 1) % NZ) + 1, 2 * i + 1)]
    return lax.ppermute(a, (Z, C), pairs)


def far(a):
    return pltpu.with_memory_space_constraint(a, pltpu.HBM)


def ring_z(a, b):
    mine, others = [a] + [None] * (NZ - 1), [b] + [None] * (NZ - 1)
    for step in range(1, 4):
        a = turn(a)
        b = turn(b)
        mine[step], others[step] = a, b
        mine[NZ - step], others[NZ - step] = swap(b), swap(a)
    mine[4] = turn(a)
    others[4] = swap(mine[4])
    return [part[e] for e in ORDER for part in (mine, others)]


def where_from(i):
    core, z = lax.axis_index(C), lax.axis_index(Z)
    e = ORDER[i // 2]
    return (z + e + core * (NZ - 2 * e) + NZ) % NZ, core if i % 2 == 0 else 1 - core


def near(a):
    return pltpu.with_memory_space_constraint(a, pltpu.VMEM)


def spread(a_ref, out_ref, sem):
    copies = [pltpu.make_async_copy(a_ref, out_ref.at[i], sem.at[i]) for i in range(NR)]
    for copy in copies:
        copy.start()
    for copy in copies:
        copy.wait()


def copies_of(a):
    return pl.pallas_call(
        spread,
        out_shape=pltpu.HBM((NR, *a.shape), a.dtype),
        in_specs=[VMEM],
        out_specs=HBM,
        scratch_shapes=[pltpu.SemaphoreType.DMA((NR,))],
        compiler_params=pltpu.CompilerParams(vmem_limit_bytes=1 << 20),
        cost_estimate=pl.CostEstimate(flops=0, bytes_accessed=5 << 20, transcendentals=0),
        name="copies",
    )(near(a))


def gather_r(copies):
    return lax.all_to_all(copies, (X, YL), 0, 0, tiled=True)


def join_kernel(own_a, got_a, own_b, got_b, gram_ref):
    for i in range(PARTS):
        z, h = where_from(i)
        if i < EARLY:
            rows = pl.ds(i * ROWS, ROWS)
            value = own_a[rows, :] + got_a[rows, :].astype(f32)
        else:
            rows = pl.ds((i - EARLY) * ROWS, ROWS)
            value = own_b[rows, :] + got_b[rows, :].astype(f32)
        gram_ref[2 * z + h] = value.astype(bf16)


def join(*parts):
    return pl.pallas_call(
        join_kernel,
        out_shape=pltpu.VMEM((PARTS, ROWS, TILE), bf16),
        in_specs=[VMEM] * 4,
        out_specs=VMEM,
        compiler_params=pltpu.CompilerParams(vmem_limit_bytes=4 << 20),
        name="join",
    )(*[near(p) for p in parts])


def gram_kernel(count, cut, *refs):
    pieces, cols_ref, own_ref, sent_ref = refs[:count], refs[count], refs[count + 1], refs[count + 2]
    x, sem = refs[-2:]
    copies = [pltpu.make_async_copy(piece, x.at[i], sem.at[i]) for i, piece in enumerate(pieces)]
    if cut:
        copies.append(pltpu.make_async_copy(cols_ref.at[:, :, pl.ds(0, COLS_Z)], refs[count + 3], sem.at[count]))
    for copy in copies:
        copy.start()
    for copy in copies[:count]:
        copy.wait()
    left = x[...].reshape(count * ROWS, COLS)
    right = cols_ref[...].reshape(TILE, COLS)
    total = lax.dot_general(left, right, (((1,), (1,)), ((), ())), preferred_element_type=f32)
    own_ref[...] = total
    sent_ref[...] = total.astype(bf16)
    for copy in copies[count:]:
        copy.wait()


def gram_part(pieces, near_from, cols, cut):
    count = len(pieces)
    n = count * ROWS
    outs = [pltpu.VMEM((n, TILE), f32), pltpu.VMEM((n, TILE), bf16)]
    if cut:
        outs.append(pltpu.HBM((NR, ROWS, COLS_Z), bf16))
    return pl.pallas_call(
        functools.partial(gram_kernel, count, cut),
        out_shape=tuple(outs),
        in_specs=[HBM] * near_from + [VMEM] * (count - near_from) + [VMEM],
        out_specs=(VMEM, VMEM, HBM)[: len(outs)],
        scratch_shapes=[
            pltpu.VMEM((count, ROWS, COLS), bf16),
            pltpu.SemaphoreType.DMA((count + 1,)),
        ],
        compiler_params=pltpu.CompilerParams(vmem_limit_bytes=10 << 20),
        cost_estimate=pl.CostEstimate(flops=2 * n * TILE * COLS, bytes_accessed=6 << 20, transcendentals=0),
        name="gram_part",
    )(*[far(p) for p in pieces[:near_from]], *[near(p) for p in pieces[near_from:]], near(cols))


def product_kernel(*refs):
    a_refs, refs = refs[:PARTS], refs[PARTS:]
    x_refs, refs = refs[:PARTS], refs[PARTS:]
    b_ref, cut_ref, out_ref, own_ref, other_ref, a, x, y, part, out, sem_a, sem_x, sem_out = refs
    copies = []
    for i, ref in enumerate(a_refs):
        z, h = where_from(i)
        at = pl.ds(i % TOGETHER * TILE, TILE)
        copies.append(pltpu.make_async_copy(ref, a.at[i // TOGETHER, :, at], sem_a.at[i]))
    loads = [pltpu.make_async_copy(cut_ref, y, sem_x.at[PARTS])]
    for i, ref in enumerate(x_refs):
        z, h = where_from(i)
        loads.append(pltpu.make_async_copy(ref.at[:, pl.ds(COLS_Z, COLS - COLS_Z)], x.at[2 * z + h], sem_x.at[i]))
    for copy in copies + loads:
        copy.start()
    squared = None
    for g in range(PARTS // TOGETHER):
        right = []
        for i in range(g * TOGETHER, (g + 1) * TOGETHER):
            z, h = where_from(i)
            copies[i].wait()
            right.append(b_ref[:, 2 * z + h].reshape(TILE, TILE))
        term = jnp.dot(a[g], jnp.concatenate(right), preferred_element_type=f32)
        squared = term if squared is None else squared + term
    gram = a[0, :, pl.ds(0, TILE)].astype(f32)
    poly = coef_cubic * gram + coef_quintic * squared
    poly_t = poly.T.astype(bf16)
    poly = poly.astype(bf16)
    loads[0].wait()
    for k in range(COLS_Z // WIDTH_Z):
        cut = pl.ds(k * WIDTH_Z, WIDTH_Z)
        term = jnp.dot(poly, y[:, :, cut].reshape(TILE, WIDTH_Z), preferred_element_type=f32)
        part[:, :, :, cut] = term.astype(bf16).reshape(NZ, 2, ROWS, WIDTH_Z)
    core, z = lax.axis_index(C), lax.axis_index(Z)
    outs = []
    for e in range(5):
        for ref, c in ((other_ref, 1 - core), (own_ref, core)):
            at = (z + e + c * (NZ - 2 * e)) % NZ
            if e in (0, 4):
                block = (part.at[at, c], ref.at[SINGLE[e]])
            else:
                block = (part.at[at], ref.at[pl.ds(2 * e - 2, 2)])
            outs.append(pltpu.make_async_copy(*block, sem_x.at[PARTS + 1 + len(outs)]))
    for copy in outs:
        copy.start()
    for load in loads[1:]:
        load.wait()
    for k in range((COLS - COLS_Z) // WIDTH):
        cut = pl.ds(k * WIDTH, WIDTH)
        right = x[:, :, cut].reshape(PARTS * ROWS, WIDTH)
        term = jnp.dot(poly_t, right, preferred_element_type=f32)
        out[:, :, cut] = term.astype(bf16).reshape(NR, ROWS, WIDTH)
        outs.append(pltpu.make_async_copy(out.at[:, :, cut], out_ref.at[:, :, cut], sem_out.at[k]))
        outs[-1].start()
    for copy in outs:
        copy.wait()


def product_part(a_parts, x_parts, b, cut):
    n = PARTS * ROWS
    return pl.pallas_call(
        product_kernel,
        out_shape=(
            pltpu.HBM((NR, ROWS, COLS - COLS_Z), bf16),
            pltpu.HBM((NZ, ROWS, COLS_Z), bf16),
            pltpu.HBM((NZ, ROWS, COLS_Z), bf16),
        ),
        in_specs=[HBM] * LATE + [VMEM] * (PARTS - LATE) + [HBM] * PARTS + [VMEM, HBM],
        out_specs=(HBM, HBM, HBM),
        scratch_shapes=[
            pltpu.VMEM((PARTS // TOGETHER, n, TOGETHER * TILE), bf16),
            pltpu.VMEM((PARTS, ROWS, COLS - COLS_Z), bf16),
            pltpu.VMEM((NR, ROWS, COLS_Z), bf16),
            pltpu.VMEM((NZ, 2, ROWS, COLS_Z), bf16),
            pltpu.VMEM((NR, ROWS, COLS - COLS_Z), bf16),
            pltpu.SemaphoreType.DMA((PARTS,)),
            pltpu.SemaphoreType.DMA((PARTS + 11,)),
            pltpu.SemaphoreType.DMA(((COLS - COLS_Z) // WIDTH,)),
        ],
        compiler_params=pltpu.CompilerParams(vmem_limit_bytes=28 << 20),
        cost_estimate=pl.CostEstimate(
            flops=2 * n * TILE * (COLS + PARTS * TILE), bytes_accessed=14 << 20, transcendentals=0
        ),
        name="product_part",
    )(*[far(p) for p in a_parts[:LATE]], *[near(p) for p in a_parts[LATE:]], *[far(p) for p in x_parts], near(b), far(cut))


def cast(a, e):
    pairs = []
    for i in range(NZ):
        pairs += [(2 * ((i - e) % NZ), 2 * i), (2 * ((i + e) % NZ) + 1, 2 * i + 1)]
    return lax.ppermute(a, (Z, C), pairs)


def on_device(iterate):
    core = lax.axis_index(C)
    copies, twin = lax.optimization_barrier((copies_of(iterate), swap(iterate)))
    cols = gather_r(copies)
    pieces = ring_z(iterate, twin)
    own_a, sent_a, cut = gram_part(pieces[:EARLY], EARLY, cols, True)
    got_a = swap_slab(sent_a)
    own_b, sent_b = gram_part(pieces[EARLY:], NEAR, cols, False)
    gram = join(own_a, got_a, own_b, swap_slab(sent_b))
    gram = gram.reshape(PARTS * ROWS, TILE)
    copies, twin = lax.optimization_barrier((copies_of(gram), swap(gram)))
    every = gather_r(copies).reshape(NR, PARTS, ROWS, TILE)
    parts, own, other = product_part(ring_z(gram, twin), pieces, every, cut)
    got = lax.all_to_all(parts, (X, YL), 0, 0, tiled=True)
    own = (own.astype(f32) + swap(other).astype(f32)).astype(bf16)
    last = cast(own[6], 4)
    pairs = [cast(own[2 * e - 2 : 2 * e], e) for e in (3, 2, 1)]
    both = sum(p.astype(f32) for p in pairs)
    here = jnp.where(core == 0, both[0], both[1])
    there = jnp.where(core == 0, both[1], both[0]).astype(bf16)
    sum_z = here + last.astype(f32) + own[7].astype(f32) + swap(there).astype(f32)
    sum_r = got.astype(f32).sum(0)
    total = coef_linear * iterate.astype(f32) + jnp.concatenate([sum_z, sum_r], axis=1)
    return (update_gain * total).astype(bf16)


def solution(mesh):
    fine = Mesh(mesh.devices.reshape(4, 2, 8, 2, 2), (X, YL, Z, C, S))
    spec = P((X, YL, Z, C), S)
    return jax.shard_map(on_device, mesh=fine, in_specs=(spec,), out_specs=spec, check_vma=False)
```

```python
import functools
import math

import jax
import jax.numpy as jnp
from jax import lax
from jax.experimental import pallas as pl
from jax.experimental.pallas import tpu as pltpu
from jax.sharding import Mesh
from jax.sharding import PartitionSpec as P

coef_linear = 3.4445
coef_cubic = -4.775
coef_quintic = 2.0315
update_gain = 0.2 * math.sqrt(18432.0)

X, YL, Z, C, S = "x", "yl", "z", "c", "s"
NZ, NR = 8, 8
ROWS, COLS = 32, 4608
TILE = 256
bf16, f32 = jnp.bfloat16, jnp.float32
ORDER = (0, 1, 7, 2, 6, 3, 5, 4)
PARTS = 16
COLS_Z = 1536
LATE = 11
EARLY = 12
NEAR = 0
WIDTH_Z, WIDTH = 768, 768
SINGLE = {4: 6, 0: 7}
TOGETHER = 2
VMEM = pl.BlockSpec(memory_space=pltpu.VMEM)
HBM = pl.BlockSpec(memory_space=pltpu.HBM)


def swap(a):
    return lax.ppermute(a, C, [(0, 1), (1, 0)])


def swap_slab(a):
    return lax.ppermute(a, S, [(0, 1), (1, 0)])


def turn(a):
    pairs = []
    for i in range(NZ):
        pairs += [(2 * ((i + 1) % NZ), 2 * i), (2 * ((i - 1) % NZ) + 1, 2 * i + 1)]
    return lax.ppermute(a, (Z, C), pairs)


def far(a):
    return pltpu.with_memory_space_constraint(a, pltpu.HBM)


def ring_z(a, b):
    mine, others = [a] + [None] * (NZ - 1), [b] + [None] * (NZ - 1)
    for step in range(1, 4):
        a = turn(a)
        b = turn(b)
        mine[step], others[step] = a, b
        mine[NZ - step], others[NZ - step] = swap(b), swap(a)
    mine[4] = turn(a)
    others[4] = swap(mine[4])
    return [part[e] for e in ORDER for part in (mine, others)]


def where_from(i):
    core, z = lax.axis_index(C), lax.axis_index(Z)
    e = ORDER[i // 2]
    return (z + e + core * (NZ - 2 * e) + NZ) % NZ, core if i % 2 == 0 else 1 - core


def near(a):
    return pltpu.with_memory_space_constraint(a, pltpu.VMEM)


def spread(a_ref, out_ref, sem):
    copies = [pltpu.make_async_copy(a_ref, out_ref.at[i], sem.at[i]) for i in range(NR)]
    for copy in copies:
        copy.start()
    for copy in copies:
        copy.wait()


def copies_of(a):
    return pl.pallas_call(
        spread,
        out_shape=pltpu.HBM((NR, *a.shape), a.dtype),
        in_specs=[VMEM],
        out_specs=HBM,
        scratch_shapes=[pltpu.SemaphoreType.DMA((NR,))],
        compiler_params=pltpu.CompilerParams(vmem_limit_bytes=1 << 20),
        cost_estimate=pl.CostEstimate(flops=0, bytes_accessed=5 << 20, transcendentals=0),
        name="copies",
    )(near(a))


def gather_r(copies):
    return lax.all_to_all(copies, (X, YL), 0, 0, tiled=True)


def join_kernel(own_a, got_a, own_b, got_b, gram_ref):
    for i in range(PARTS):
        z, h = where_from(i)
        if i < EARLY:
            rows = pl.ds(i * ROWS, ROWS)
            value = own_a[rows, :] + got_a[rows, :].astype(f32)
        else:
            rows = pl.ds((i - EARLY) * ROWS, ROWS)
            value = own_b[rows, :] + got_b[rows, :].astype(f32)
        gram_ref[2 * z + h] = value.astype(bf16)


def join(*parts):
    return pl.pallas_call(
        join_kernel,
        out_shape=pltpu.VMEM((PARTS, ROWS, TILE), bf16),
        in_specs=[VMEM] * 4,
        out_specs=VMEM,
        compiler_params=pltpu.CompilerParams(vmem_limit_bytes=4 << 20),
        name="join",
    )(*[near(p) for p in parts])


def gram_kernel(count, cut, *refs):
    pieces, cols_ref, own_ref, sent_ref = refs[:count], refs[count], refs[count + 1], refs[count + 2]
    x, sem = refs[-2:]
    copies = [pltpu.make_async_copy(piece, x.at[i], sem.at[i]) for i, piece in enumerate(pieces)]
    if cut:
        copies.append(pltpu.make_async_copy(cols_ref.at[:, :, pl.ds(0, COLS_Z)], refs[count + 3], sem.at[count]))
    for copy in copies:
        copy.start()
    for copy in copies[:count]:
        copy.wait()
    left = x[...].reshape(count * ROWS, COLS)
    right = cols_ref[...].reshape(TILE, COLS)
    total = lax.dot_general(left, right, (((1,), (1,)), ((), ())), preferred_element_type=f32)
    own_ref[...] = total
    sent_ref[...] = total.astype(bf16)
    for copy in copies[count:]:
        copy.wait()


def gram_part(pieces, near_from, cols, cut):
    count = len(pieces)
    n = count * ROWS
    outs = [pltpu.VMEM((n, TILE), f32), pltpu.VMEM((n, TILE), bf16)]
    if cut:
        outs.append(pltpu.HBM((NR, ROWS, COLS_Z), bf16))
    return pl.pallas_call(
        functools.partial(gram_kernel, count, cut),
        out_shape=tuple(outs),
        in_specs=[HBM] * near_from + [VMEM] * (count - near_from) + [VMEM],
        out_specs=(VMEM, VMEM, HBM)[: len(outs)],
        scratch_shapes=[
            pltpu.VMEM((count, ROWS, COLS), bf16),
            pltpu.SemaphoreType.DMA((count + 1,)),
        ],
        compiler_params=pltpu.CompilerParams(vmem_limit_bytes=10 << 20),
        cost_estimate=pl.CostEstimate(flops=2 * n * TILE * COLS, bytes_accessed=6 << 20, transcendentals=0),
        name="gram_part",
    )(*[far(p) for p in pieces[:near_from]], *[near(p) for p in pieces[near_from:]], near(cols))


def product_kernel(*refs):
    a_refs, refs = refs[:PARTS], refs[PARTS:]
    x_refs, refs = refs[:PARTS], refs[PARTS:]
    b_ref, cut_ref, out_ref, own_ref, other_ref, a, x, y, part, out, sem_a, sem_x, sem_out = refs
    copies = []
    for i, ref in enumerate(a_refs):
        z, h = where_from(i)
        at = pl.ds(i % TOGETHER * TILE, TILE)
        copies.append(pltpu.make_async_copy(ref, a.at[i // TOGETHER, :, at], sem_a.at[i]))
    loads = [pltpu.make_async_copy(cut_ref, y, sem_x.at[PARTS])]
    for i, ref in enumerate(x_refs):
        z, h = where_from(i)
        loads.append(pltpu.make_async_copy(ref.at[:, pl.ds(COLS_Z, COLS - COLS_Z)], x.at[2 * z + h], sem_x.at[i]))
    for copy in copies + loads:
        copy.start()
    squared = None
    for g in range(PARTS // TOGETHER):
        right = []
        for i in range(g * TOGETHER, (g + 1) * TOGETHER):
            z, h = where_from(i)
            copies[i].wait()
            right.append(b_ref[:, 2 * z + h].reshape(TILE, TILE))
        term = jnp.dot(a[g], jnp.concatenate(right), preferred_element_type=f32)
        squared = term if squared is None else squared + term
    gram = a[0, :, pl.ds(0, TILE)].astype(f32)
    poly = (coef_cubic * gram + coef_quintic * squared).astype(bf16)
    poly_t = poly.T
    loads[0].wait()
    for k in range(COLS_Z // WIDTH_Z):
        cut = pl.ds(k * WIDTH_Z, WIDTH_Z)
        term = jnp.dot(poly, y[:, :, cut].reshape(TILE, WIDTH_Z), preferred_element_type=f32)
        part[:, :, :, cut] = term.astype(bf16).reshape(NZ, 2, ROWS, WIDTH_Z)
    core, z = lax.axis_index(C), lax.axis_index(Z)
    outs = []
    for e in range(5):
        for ref, c in ((other_ref, 1 - core), (own_ref, core)):
            at = (z + e + c * (NZ - 2 * e)) % NZ
            if e in (0, 4):
                block = (part.at[at, c], ref.at[SINGLE[e]])
            else:
                block = (part.at[at], ref.at[pl.ds(2 * e - 2, 2)])
            outs.append(pltpu.make_async_copy(*block, sem_x.at[PARTS + 1 + len(outs)]))
    for copy in outs:
        copy.start()
    for load in loads[1:]:
        load.wait()
    for k in range((COLS - COLS_Z) // WIDTH):
        cut = pl.ds(k * WIDTH, WIDTH)
        right = x[:, :, cut].reshape(PARTS * ROWS, WIDTH)
        term = jnp.dot(poly_t, right, preferred_element_type=f32)
        out[:, :, cut] = term.astype(bf16).reshape(NR, ROWS, WIDTH)
        outs.append(pltpu.make_async_copy(out.at[:, :, cut], out_ref.at[:, :, cut], sem_out.at[k]))
        outs[-1].start()
    for copy in outs:
        copy.wait()


def product_part(a_parts, x_parts, b, cut):
    n = PARTS * ROWS
    return pl.pallas_call(
        product_kernel,
        out_shape=(
            pltpu.HBM((NR, ROWS, COLS - COLS_Z), bf16),
            pltpu.HBM((NZ, ROWS, COLS_Z), bf16),
            pltpu.HBM((NZ, ROWS, COLS_Z), bf16),
        ),
        in_specs=[HBM] * LATE + [VMEM] * (PARTS - LATE) + [HBM] * PARTS + [VMEM, HBM],
        out_specs=(HBM, HBM, HBM),
        scratch_shapes=[
            pltpu.VMEM((PARTS // TOGETHER, n, TOGETHER * TILE), bf16),
            pltpu.VMEM((PARTS, ROWS, COLS - COLS_Z), bf16),
            pltpu.VMEM((NR, ROWS, COLS_Z), bf16),
            pltpu.VMEM((NZ, 2, ROWS, COLS_Z), bf16),
            pltpu.VMEM((NR, ROWS, COLS - COLS_Z), bf16),
            pltpu.SemaphoreType.DMA((PARTS,)),
            pltpu.SemaphoreType.DMA((PARTS + 11,)),
            pltpu.SemaphoreType.DMA(((COLS - COLS_Z) // WIDTH,)),
        ],
        compiler_params=pltpu.CompilerParams(vmem_limit_bytes=28 << 20),
        cost_estimate=pl.CostEstimate(
            flops=2 * n * TILE * (COLS + PARTS * TILE), bytes_accessed=14 << 20, transcendentals=0
        ),
        name="product_part",
    )(*[far(p) for p in a_parts[:LATE]], *[near(p) for p in a_parts[LATE:]], *[far(p) for p in x_parts], near(b), far(cut))


def cast(a, e):
    pairs = []
    for i in range(NZ):
        pairs += [(2 * ((i - e) % NZ), 2 * i), (2 * ((i + e) % NZ) + 1, 2 * i + 1)]
    return lax.ppermute(a, (Z, C), pairs)


def on_device(iterate):
    core = lax.axis_index(C)
    copies, twin = lax.optimization_barrier((copies_of(iterate), swap(iterate)))
    cols = gather_r(copies)
    pieces = ring_z(iterate, twin)
    own_a, sent_a, cut = gram_part(pieces[:EARLY], EARLY, cols, True)
    got_a = swap_slab(sent_a)
    own_b, sent_b = gram_part(pieces[EARLY:], NEAR, cols, False)
    gram = join(own_a, got_a, own_b, swap_slab(sent_b))
    gram = gram.reshape(PARTS * ROWS, TILE)
    copies, twin = lax.optimization_barrier((copies_of(gram), swap(gram)))
    every = gather_r(copies).reshape(NR, PARTS, ROWS, TILE)
    parts, own, other = product_part(ring_z(gram, twin), pieces, every, cut)
    got = lax.all_to_all(parts, (X, YL), 0, 0, tiled=True)
    own = (own.astype(f32) + swap(other).astype(f32)).astype(bf16)
    last = cast(own[6], 4)
    pairs = [cast(own[2 * e - 2 : 2 * e], e) for e in (3, 2, 1)]
    both = sum(p.astype(f32) for p in pairs)
    here = jnp.where(core == 0, both[0], both[1])
    there = jnp.where(core == 0, both[1], both[0]).astype(bf16)
    sum_z = here + last.astype(f32) + own[7].astype(f32) + swap(there).astype(f32)
    sum_r = got.astype(f32).sum(0)
    total = coef_linear * iterate.astype(f32) + jnp.concatenate([sum_z, sum_r], axis=1)
    return (update_gain * total).astype(bf16)


def solution(mesh):
    fine = Mesh(mesh.devices.reshape(4, 2, 8, 2, 2), (X, YL, Z, C, S))
    spec = P((X, YL, Z, C), S)
    return jax.shard_map(on_device, mesh=fine, in_specs=(spec,), out_specs=spec, check_vma=False)
```

```python
import functools
import math

import jax
import jax.numpy as jnp
from jax import lax
from jax.experimental import pallas as pl
from jax.experimental.pallas import tpu as pltpu
from jax.sharding import Mesh
from jax.sharding import PartitionSpec as P

coef_linear = 3.4445
coef_cubic = -4.775
coef_quintic = 2.0315
update_gain = 0.2 * math.sqrt(18432.0)

X, YL, Z, C, S = "x", "yl", "z", "c", "s"
NZ, NR = 8, 8
ROWS, COLS = 32, 4608
TILE = 256
bf16, f32 = jnp.bfloat16, jnp.float32
ORDER = (0, 1, 7, 2, 6, 3, 5, 4)
PARTS = 16
COLS_Z = 1536
LATE = 11
EARLY = 12
NEAR = 0
WIDTH_Z, WIDTH = 768, 768
SINGLE = {4: 6, 0: 7}
TOGETHER = 2
VMEM = pl.BlockSpec(memory_space=pltpu.VMEM)
HBM = pl.BlockSpec(memory_space=pltpu.HBM)


def swap(a):
    return lax.ppermute(a, C, [(0, 1), (1, 0)])


def swap_slab(a):
    return lax.ppermute(a, S, [(0, 1), (1, 0)])


def turn(a):
    pairs = []
    for i in range(NZ):
        pairs += [(2 * ((i + 1) % NZ), 2 * i), (2 * ((i - 1) % NZ) + 1, 2 * i + 1)]
    return lax.ppermute(a, (Z, C), pairs)


def far(a):
    return pltpu.with_memory_space_constraint(a, pltpu.HBM)


def ring_z(a, b):
    mine, others = [a] + [None] * (NZ - 1), [b] + [None] * (NZ - 1)
    for step in range(1, 4):
        a = turn(a)
        b = turn(b)
        mine[step], others[step] = a, b
        mine[NZ - step], others[NZ - step] = swap(b), swap(a)
    mine[4] = turn(a)
    others[4] = swap(mine[4])
    return [part[e] for e in ORDER for part in (mine, others)]


def where_from(i):
    core, z = lax.axis_index(C), lax.axis_index(Z)
    e = ORDER[i // 2]
    return (z + e + core * (NZ - 2 * e) + NZ) % NZ, core if i % 2 == 0 else 1 - core


def near(a):
    return pltpu.with_memory_space_constraint(a, pltpu.VMEM)


def spread(a_ref, out_ref, sem):
    copies = [pltpu.make_async_copy(a_ref, out_ref.at[i], sem.at[i]) for i in range(NR)]
    for copy in copies:
        copy.start()
    for copy in copies:
        copy.wait()


def copies_of(a):
    return pl.pallas_call(
        spread,
        out_shape=pltpu.HBM((NR, *a.shape), a.dtype),
        in_specs=[VMEM],
        out_specs=HBM,
        scratch_shapes=[pltpu.SemaphoreType.DMA((NR,))],
        compiler_params=pltpu.CompilerParams(vmem_limit_bytes=1 << 20),
        cost_estimate=pl.CostEstimate(flops=0, bytes_accessed=5 << 20, transcendentals=0),
        name="copies",
    )(near(a))


def gather_r(copies):
    return lax.all_to_all(copies, (X, YL), 0, 0, tiled=True)


def join_kernel(own_a, got_a, own_b, got_b, gram_ref):
    for i in range(PARTS):
        z, h = where_from(i)
        if i < EARLY:
            rows = pl.ds(i * ROWS, ROWS)
            value = own_a[rows, :] + got_a[rows, :].astype(f32)
        else:
            rows = pl.ds((i - EARLY) * ROWS, ROWS)
            value = own_b[rows, :] + got_b[rows, :].astype(f32)
        gram_ref[2 * z + h] = value.astype(bf16)


def join(*parts):
    return pl.pallas_call(
        join_kernel,
        out_shape=pltpu.VMEM((PARTS, ROWS, TILE), bf16),
        in_specs=[VMEM] * 4,
        out_specs=VMEM,
        compiler_params=pltpu.CompilerParams(vmem_limit_bytes=4 << 20),
        name="join",
    )(*[near(p) for p in parts])


def gram_kernel(count, cut, *refs):
    pieces, cols_ref, own_ref, sent_ref = refs[:count], refs[count], refs[count + 1], refs[count + 2]
    x, sem = refs[-2:]
    copies = [pltpu.make_async_copy(piece, x.at[i], sem.at[i]) for i, piece in enumerate(pieces)]
    if cut:
        copies.append(pltpu.make_async_copy(cols_ref.at[:, :, pl.ds(0, COLS_Z)], refs[count + 3], sem.at[count]))
    for copy in copies:
        copy.start()
    for copy in copies[:count]:
        copy.wait()
    left = x[...].reshape(count * ROWS, COLS)
    right = cols_ref[...].reshape(TILE, COLS)
    over_columns = (((1,), (1,)), ((), ()))
    if count * ROWS < TILE:
        total = lax.dot_general(right, left, over_columns, preferred_element_type=f32).T
    else:
        total = lax.dot_general(left, right, over_columns, preferred_element_type=f32)
    own_ref[...] = total
    sent_ref[...] = total.astype(bf16)
    for copy in copies[count:]:
        copy.wait()


def gram_part(pieces, near_from, cols, cut):
    count = len(pieces)
    n = count * ROWS
    outs = [pltpu.VMEM((n, TILE), f32), pltpu.VMEM((n, TILE), bf16)]
    if cut:
        outs.append(pltpu.HBM((NR, ROWS, COLS_Z), bf16))
    return pl.pallas_call(
        functools.partial(gram_kernel, count, cut),
        out_shape=tuple(outs),
        in_specs=[HBM] * near_from + [VMEM] * (count - near_from) + [VMEM],
        out_specs=(VMEM, VMEM, HBM)[: len(outs)],
        scratch_shapes=[
            pltpu.VMEM((count, ROWS, COLS), bf16),
            pltpu.SemaphoreType.DMA((count + 1,)),
        ],
        compiler_params=pltpu.CompilerParams(vmem_limit_bytes=10 << 20),
        cost_estimate=pl.CostEstimate(flops=2 * n * TILE * COLS, bytes_accessed=6 << 20, transcendentals=0),
        name="gram_part",
    )(*[far(p) for p in pieces[:near_from]], *[near(p) for p in pieces[near_from:]], near(cols))


def product_kernel(*refs):
    a_refs, refs = refs[:PARTS], refs[PARTS:]
    x_refs, refs = refs[:PARTS], refs[PARTS:]
    b_ref, cut_ref, out_ref, own_ref, other_ref, a, x, y, part, out, sem_a, sem_x, sem_out = refs
    copies = []
    for i, ref in enumerate(a_refs):
        z, h = where_from(i)
        at = pl.ds(i % TOGETHER * TILE, TILE)
        copies.append(pltpu.make_async_copy(ref, a.at[i // TOGETHER, :, at], sem_a.at[i]))
    loads = [pltpu.make_async_copy(cut_ref, y, sem_x.at[PARTS])]
    for i, ref in enumerate(x_refs):
        z, h = where_from(i)
        loads.append(pltpu.make_async_copy(ref.at[:, pl.ds(COLS_Z, COLS - COLS_Z)], x.at[2 * z + h], sem_x.at[i]))
    for copy in copies + loads:
        copy.start()
    squared = None
    for g in range(PARTS // TOGETHER):
        right = []
        for i in range(g * TOGETHER, (g + 1) * TOGETHER):
            z, h = where_from(i)
            copies[i].wait()
            right.append(b_ref[:, 2 * z + h].reshape(TILE, TILE))
        term = jnp.dot(a[g], jnp.concatenate(right), preferred_element_type=f32)
        squared = term if squared is None else squared + term
    gram = a[0, :, pl.ds(0, TILE)].astype(f32)
    poly = coef_cubic * gram + coef_quintic * squared
    poly_t = poly.T.astype(bf16)
    poly = poly.astype(bf16)
    loads[0].wait()
    for k in range(COLS_Z // WIDTH_Z):
        cut = pl.ds(k * WIDTH_Z, WIDTH_Z)
        term = jnp.dot(poly, y[:, :, cut].reshape(TILE, WIDTH_Z), preferred_element_type=f32)
        part[:, :, :, cut] = term.astype(bf16).reshape(NZ, 2, ROWS, WIDTH_Z)
    core, z = lax.axis_index(C), lax.axis_index(Z)
    outs = []
    for e in range(5):
        for ref, c in ((other_ref, 1 - core), (own_ref, core)):
            at = (z + e + c * (NZ - 2 * e)) % NZ
            if e in (0, 4):
                block = (part.at[at, c], ref.at[SINGLE[e]])
            else:
                block = (part.at[at], ref.at[pl.ds(2 * e - 2, 2)])
            outs.append(pltpu.make_async_copy(*block, sem_x.at[PARTS + 1 + len(outs)]))
    for copy in outs:
        copy.start()
    for load in loads[1:]:
        load.wait()
    for k in range((COLS - COLS_Z) // WIDTH):
        cut = pl.ds(k * WIDTH, WIDTH)
        right = x[:, :, cut].reshape(PARTS * ROWS, WIDTH)
        term = jnp.dot(poly_t, right, preferred_element_type=f32)
        out[:, :, cut] = term.astype(bf16).reshape(NR, ROWS, WIDTH)
        outs.append(pltpu.make_async_copy(out.at[:, :, cut], out_ref.at[:, :, cut], sem_out.at[k]))
        outs[-1].start()
    for copy in outs:
        copy.wait()


def product_part(a_parts, x_parts, b, cut):
    n = PARTS * ROWS
    return pl.pallas_call(
        product_kernel,
        out_shape=(
            pltpu.HBM((NR, ROWS, COLS - COLS_Z), bf16),
            pltpu.HBM((NZ, ROWS, COLS_Z), bf16),
            pltpu.HBM((NZ, ROWS, COLS_Z), bf16),
        ),
        in_specs=[HBM] * LATE + [VMEM] * (PARTS - LATE) + [HBM] * PARTS + [VMEM, HBM],
        out_specs=(HBM, HBM, HBM),
        scratch_shapes=[
            pltpu.VMEM((PARTS // TOGETHER, n, TOGETHER * TILE), bf16),
            pltpu.VMEM((PARTS, ROWS, COLS - COLS_Z), bf16),
            pltpu.VMEM((NR, ROWS, COLS_Z), bf16),
            pltpu.VMEM((NZ, 2, ROWS, COLS_Z), bf16),
            pltpu.VMEM((NR, ROWS, COLS - COLS_Z), bf16),
            pltpu.SemaphoreType.DMA((PARTS,)),
            pltpu.SemaphoreType.DMA((PARTS + 11,)),
            pltpu.SemaphoreType.DMA(((COLS - COLS_Z) // WIDTH,)),
        ],
        compiler_params=pltpu.CompilerParams(vmem_limit_bytes=28 << 20),
        cost_estimate=pl.CostEstimate(
            flops=2 * n * TILE * (COLS + PARTS * TILE), bytes_accessed=14 << 20, transcendentals=0
        ),
        name="product_part",
    )(*[far(p) for p in a_parts[:LATE]], *[near(p) for p in a_parts[LATE:]], *[far(p) for p in x_parts], near(b), far(cut))


def cast(a, e):
    pairs = []
    for i in range(NZ):
        pairs += [(2 * ((i - e) % NZ), 2 * i), (2 * ((i + e) % NZ) + 1, 2 * i + 1)]
    return lax.ppermute(a, (Z, C), pairs)


def on_device(iterate):
    core = lax.axis_index(C)
    copies, twin = lax.optimization_barrier((copies_of(iterate), swap(iterate)))
    cols = gather_r(copies)
    pieces = ring_z(iterate, twin)
    own_a, sent_a, cut = gram_part(pieces[:EARLY], EARLY, cols, True)
    got_a = swap_slab(sent_a)
    own_b, sent_b = gram_part(pieces[EARLY:], NEAR, cols, False)
    gram = join(own_a, got_a, own_b, swap_slab(sent_b))
    gram = gram.reshape(PARTS * ROWS, TILE)
    copies, twin = lax.optimization_barrier((copies_of(gram), swap(gram)))
    every = gather_r(copies).reshape(NR, PARTS, ROWS, TILE)
    parts, own, other = product_part(ring_z(gram, twin), pieces, every, cut)
    got = lax.all_to_all(parts, (X, YL), 0, 0, tiled=True)
    own = (own.astype(f32) + swap(other).astype(f32)).astype(bf16)
    last = cast(own[6], 4)
    pairs = [cast(own[2 * e - 2 : 2 * e], e) for e in (3, 2, 1)]
    both = sum(p.astype(f32) for p in pairs)
    here = jnp.where(core == 0, both[0], both[1])
    there = jnp.where(core == 0, both[1], both[0]).astype(bf16)
    sum_z = here + last.astype(f32) + own[7].astype(f32) + swap(there).astype(f32)
    sum_r = got.astype(f32).sum(0)
    total = coef_linear * iterate.astype(f32) + jnp.concatenate([sum_z, sum_r], axis=1)
    return (update_gain * total).astype(bf16)


def solution(mesh):
    fine = Mesh(mesh.devices.reshape(4, 2, 8, 2, 2), (X, YL, Z, C, S))
    spec = P((X, YL, Z, C), S)
    return jax.shard_map(on_device, mesh=fine, in_specs=(spec,), out_specs=spec, check_vma=False)
```
